512 devices in a mesh: dom: 32 (over x_hi, z), pan: 16 (over y, x_lo, core).
Axes of the slice: x: 4 (x_hi: 2, x_lo: 2; x = x_hi * 2 + x_lo), y: 4, z: 16, core: 2. Of those that a mesh axis runs over, the one named last changes fastest.
Arguments:
- coupling_tiles: bfloat16 [512, 8, 256, 256], P(('dom', 'pan')), may hold values from -6 to 6
- coupling_cols: int32 [512, 8], P(('dom', 'pan')), may hold values from 0 to 255, as said below
- row_blocks: int32 [512], P(('dom', 'pan')), may hold values from 0 to 15, as said below
- factor_tiles: bfloat16 [8192, 256, 256], P(('dom', 'pan')), as said below
Outputs:
- refined_tiles: bfloat16 [512, 8, 256, 256], P(('dom', 'pan'))
The draws below stay inside these ranges and needn't reach their ends.
Inputs may be any that keep to these rules, and one draw needn't show every extreme that they name: `coupling_cols`: A row on a device of pan index p names only blocks held by pan indices p - 1, p, p + 1 of the sibling, that is values from max(p - 1, 0) * 16 to (min(p + 1, 15) + 1) * 16 - 1; every device names blocks of both neighbouring pan indices where they exist. `row_blocks`: the rows of one device name distinct blocks. `factor_tiles`: each tile is upper triangular with a positive diagonal.
All inputs are finite; a program needn't handle non-finite values.
Results may differ from the reference program's by a relative error of at most 0.0053.
Values may be sent and summed in bfloat16 or wider, within the bound.
No kernel may reach another device: no remote copies, remote signals or barrier semaphores. Data moves between devices by JAX's collectives and lax.ppermute only.
A program may use at most 64 MiB of HBM per device.

```python
import jax
import jax.numpy as jnp
from jax import lax

W = 256
NB = 16
R = 1
K = 8
ROWS = 512
N_DOM = 32
N_PAN = 16


def draw_coupling_cols(key, part):
    key = jax.random.fold_in(key, 11)
    total_rows = R * N_DOM * N_PAN
    first_key, second_key = jax.random.split(key)
    offsets = jax.random.randint(first_key, (total_rows, K), -1, 2)
    row_index = jnp.arange(total_rows, dtype=jnp.int32)[:, None]
    slot_index = jnp.arange(K, dtype=jnp.int32)[None, :]
    leading = row_index % R == 0
    offsets = jnp.where(leading & (slot_index == 0), -1, offsets)
    offsets = jnp.where(leading & (slot_index == 1), 1, offsets)
    panel = row_index // R % N_PAN
    target = jnp.clip(panel + offsets, 0, N_PAN - 1)
    within = jax.random.randint(second_key, (total_rows, K), 0, NB)
    within = jnp.where((row_index == 0) & (slot_index == 0), 0, within)
    within = jnp.where((row_index == total_rows - 1) & (slot_index == 1), NB - 1, within)
    return (target * NB + within).astype(jnp.int32)


def draw_row_blocks(key, part):
    key = jax.random.fold_in(key, 12)
    keys = jax.random.split(key, N_DOM * N_PAN)
    orders = jax.vmap(lambda single: jax.random.permutation(single, NB))(keys)
    return orders[:, :R].reshape(-1).astype(jnp.int32)


def draw_factor_tiles(key, part):
    key = jax.random.fold_in(key, 13)
    first_key, second_key = jax.random.split(key)
    shape = (NB * N_DOM * N_PAN, W, W)
    rows = jnp.arange(W, dtype=jnp.int32)[:, None]
    cols = jnp.arange(W, dtype=jnp.int32)[None, :]
    upper = (cols > rows).astype(jnp.float32)
    diag = (cols == rows).astype(jnp.float32)
    off = jax.random.normal(first_key, shape, jnp.float32) * W ** (-0.5)
    main = jax.random.uniform(second_key, shape, jnp.float32, 0.8, 1.25)
    return (off * upper + main * diag).astype(jnp.bfloat16)


def level_of(key, dims, cuts, smallest, high):
    loudness, own = 1.0, jax.random.fold_in(key, 6)
    for position, shards_of in cuts:
        steps = jnp.exp(jax.random.uniform(jax.random.fold_in(own, position), (shards_of,), jnp.float32, smallest / len(cuts), high / len(cuts)))
        loudness = loudness * jnp.repeat(steps, dims[position] // shards_of).reshape([-1 if axis == position else 1 for axis in range(len(dims))])
    return loudness


def scatter_about(rng, extent, scale, limit, pieces=(), held_as=jnp.bfloat16):
    gain = level_of(rng, extent, pieces, -0.22, 0.18) if pieces else 1.0
    result = jax.random.normal(rng, extent, jnp.float32) * scale * gain
    return jnp.minimum(jnp.maximum(result, -limit), limit).astype(held_as)


def setup_inputs(seed: int = 0) -> dict:
    splits = jax.random.split(jax.random.key(seed), 5)
    coupling_tiles = scatter_about(splits[0], (ROWS, K, W, W), 1.0, 6.0, ((0, 512),))
    coupling_cols = draw_coupling_cols(jax.random.fold_in(splits[4], 71), 0)
    row_blocks = draw_row_blocks(jax.random.fold_in(splits[4], 71), 0)
    factor_tiles = draw_factor_tiles(jax.random.fold_in(splits[4], 71), 0)
    return {"coupling_tiles": coupling_tiles, "coupling_cols": coupling_cols, "row_blocks": row_blocks, "factor_tiles": factor_tiles}


def reference(coupling_tiles, coupling_cols, row_blocks, factor_tiles):
    row_ids = jnp.arange(R * N_DOM * N_PAN, dtype=jnp.int32)

    def one_row(item):
        tiles, cols, own, index = item
        device = index // R
        dom_index = device // N_PAN
        sibling = jnp.bitwise_xor(dom_index, jnp.int32(N_DOM // 2))
        base = (sibling * N_PAN * NB).astype(jnp.int32)
        z_row = jnp.take(factor_tiles, (device * NB + own).astype(jnp.int32), axis=0).astype(jnp.float32)
        z_cols = jnp.take(factor_tiles, (base + cols).astype(jnp.int32), axis=0).astype(jnp.float32)
        left = jnp.einsum('ab,kac->kbc', z_row, tiles.astype(jnp.float32)).astype(jnp.bfloat16)
        inner = jnp.einsum('kab,kbc->kac', left.astype(jnp.float32), z_cols).astype(jnp.bfloat16)
        return (-0.5 * jnp.einsum('ab,kbc->kac', z_row, inner.astype(jnp.float32))).astype(jnp.bfloat16)

    return lax.map(one_row, (coupling_tiles, coupling_cols, row_blocks, row_ids))
```

```python
import functools

import jax
import jax.numpy as jnp
from jax import lax
from jax.experimental import pallas as pl
from jax.experimental.pallas import tpu as pltpu
from jax.sharding import PartitionSpec as P


def other_panel(panel, panels):
    there = panel + 2 * (panel % 2) - 1
    return there if 0 <= there < panels else panel


def slots_of(cols_ref, panel, blocks, put):
    count = cols_ref.shape[1]
    near_used = jnp.int32(0)
    far_used = jnp.int32(0)
    for k in range(count):
        col = cols_ref[0, k]
        near = (lax.div(col, 2 * blocks) == lax.div(panel, 2)) & (near_used < count - 1)
        put(k, col, near, jnp.where(near, near_used, far_used))
        near_used = near_used + near.astype(jnp.int32)
        far_used = far_used + 1 - near.astype(jnp.int32)


def pack_kernel(panels, near_cols, far_cols, own, mate, near_out, far_out, source, tiles, sems):
    blocks, width, _ = own.shape
    half = width // 2
    slots = tiles.shape[0] // 2
    me = lax.axis_index("pan")
    odd = lax.rem(me, 2)
    there = me + 2 * odd - 1
    there = jnp.where((there < 0) | (there >= panels), me, there)
    for slot in range(2 * slots):
        source[slot] = jnp.int32(0)

    def local(col):
        return lax.rem(col, blocks) + jnp.where(lax.div(col, blocks) == me, 0, blocks)

    def put_near(k, col, near, slot):
        @pl.when(near)
        def _():
            source[slot] = local(col)

    def put_far(k, col, near, slot):
        @pl.when(jnp.logical_not(near))
        def _():
            source[slots + slot] = local(col)

    slots_of(near_cols, me, blocks, put_near)
    slots_of(far_cols, there, blocks, put_far)

    for slot in range(2 * slots):
        index = source[slot]

        @pl.when(index < blocks)
        def _():
            pltpu.make_async_copy(own.at[index], tiles.at[slot], sems.at[slot]).start()

        @pl.when(index >= blocks)
        def _():
            pltpu.make_async_copy(mate.at[index - blocks], tiles.at[slot], sems.at[slot]).start()

    rows = lax.broadcasted_iota(jnp.int32, (half, half), 0)
    lanes = lax.broadcasted_iota(jnp.int32, (half, half), 1)
    line = lax.broadcasted_iota(jnp.int32, (16, half), 0)
    for out, first in ((near_out, 0), (far_out, slots)):
        diagonals = jnp.zeros((16, half), jnp.float32)
        for slot in range(slots):
            pltpu.make_async_copy(own.at[0], tiles.at[first + slot], sems.at[first + slot]).wait()
            upper = tiles[first + slot, :half, :half].astype(jnp.float32)
            lower = tiles[first + slot, half:, half:].astype(jnp.float32)
            base = slot * width
            out[base : base + half, :] = jnp.where(rows <= lanes, upper, lower.T).astype(jnp.bfloat16)
            out[base + half : base + width, :] = tiles[first + slot, :half, half:]
            diagonal = jnp.sum(jnp.where(rows == lanes, lower, 0.0), axis=0, keepdims=True)
            diagonals = jnp.where(line == slot, diagonal, diagonals)
        out[slots * width :, :] = diagonals.astype(jnp.bfloat16)


def left_kernel(block, factors, tiles, left, z_row, sem):
    copy = pltpu.make_async_copy(factors.at[block[0]], z_row, sem)
    copy.start()
    copy.wait()
    turned = z_row[...].astype(jnp.float32).T.astype(jnp.bfloat16)
    for k in range(tiles.shape[1]):
        left[k] = jnp.dot(turned, tiles[0, k], preferred_element_type=jnp.float32).astype(jnp.bfloat16)


def right_kernel(blocks, cols, near, far, left, z_row, out, z_col):
    slots = left.shape[0] - 1
    width = z_row.shape[0]
    half = width // 2
    me = lax.axis_index("pan")
    rows = lax.broadcasted_iota(jnp.int32, (half, half), 0)
    lanes = lax.broadcasted_iota(jnp.int32, (half, half), 1)
    line = lax.broadcasted_iota(jnp.int32, (16, half), 0)
    z_col[half:, :half] = jnp.zeros((half, half), jnp.bfloat16)

    def one(k, col, is_near, slot):
        def unpack(source):
            base = pl.multiple_of(slot * width, width)
            packed = source[pl.ds(base, half), :].astype(jnp.float32)
            diagonals = source[slots * width :, :].astype(jnp.float32)
            diagonal = jnp.sum(jnp.where(line == slot, diagonals, 0.0), axis=0, keepdims=True)
            z_col[:half, :half] = jnp.where(rows <= lanes, packed, 0.0).astype(jnp.bfloat16)
            z_col[:half, half:] = source[pl.ds(base + half, half), :]
            lower = jnp.where(rows < lanes, packed.T, jnp.where(rows == lanes, diagonal, 0.0))
            z_col[half:, half:] = lower.astype(jnp.bfloat16)

        @pl.when(is_near)
        def _():
            unpack(near)

        @pl.when(jnp.logical_not(is_near))
        def _():
            unpack(far)

        inner = jnp.dot(left[k], z_col[...], preferred_element_type=jnp.float32).astype(jnp.bfloat16)
        product = jnp.dot(z_row[...], inner, preferred_element_type=jnp.float32)
        out[0, k] = (-0.5 * product).astype(jnp.bfloat16)

    slots_of(cols, me, blocks, one)


VMEM = pl.BlockSpec(memory_space=pltpu.VMEM)
SMEM = pl.BlockSpec(memory_space=pltpu.SMEM)
ANY = pl.BlockSpec(memory_space=pl.ANY)


def on_device(coupling_tiles, coupling_cols, row_blocks, factor_tiles):
    doms, panels = lax.axis_size("dom"), lax.axis_size("pan")
    blocks, width, _ = factor_tiles.shape
    _, count, _, _ = coupling_tiles.shape
    half, slots = width // 2, count - 1
    limit = pltpu.CompilerParams(vmem_limit_bytes=24 * 2**20)

    def flat(dom, panel):
        return dom * panels + panel

    straight = [(dom, dom ^ (doms // 2)) for dom in range(doms)]
    across = [
        (flat(dom, panel), flat(dom ^ (doms // 2), other_panel(panel, panels)))
        for dom in range(doms)
        for panel in range(panels)
    ]
    near_cols = lax.ppermute(coupling_cols, "dom", straight)
    far_cols = lax.ppermute(coupling_cols, ("dom", "pan"), across)
    mate = lax.ppermute(factor_tiles, "pan", [(panel, panel ^ 1) for panel in range(panels)])

    message = jax.ShapeDtypeStruct((slots * width + 16, half), jnp.bfloat16)
    near, far = pl.pallas_call(
        functools.partial(pack_kernel, panels),
        out_shape=(message, message),
        in_specs=[SMEM, SMEM, ANY, ANY],
        out_specs=(VMEM, VMEM),
        scratch_shapes=[
            pltpu.SMEM((2 * slots,), jnp.int32),
            pltpu.VMEM((2 * slots, width, width), jnp.bfloat16),
            pltpu.SemaphoreType.DMA((2 * slots,)),
        ],
        compiler_params=limit,
        name="pack",
    )(near_cols, far_cols, factor_tiles, mate)
    far = lax.ppermute(far, ("dom", "pan"), across)
    near = lax.ppermute(near, "dom", straight)

    square = jax.ShapeDtypeStruct((width, width), jnp.bfloat16)
    left, z_row = pl.pallas_call(
        left_kernel,
        out_shape=(jax.ShapeDtypeStruct((count, width, width), jnp.bfloat16), square),
        in_specs=[SMEM, ANY, VMEM],
        out_specs=(VMEM, VMEM),
        scratch_shapes=[pltpu.SemaphoreType.DMA],
        compiler_params=limit,
        cost_estimate=pl.CostEstimate(
            flops=2 * count * width**3, bytes_accessed=4 * count * width**2, transcendentals=0
        ),
        name="left",
    )(row_blocks, factor_tiles, coupling_tiles)

    return pl.pallas_call(
        functools.partial(right_kernel, blocks),
        out_shape=jax.ShapeDtypeStruct(coupling_tiles.shape, jnp.bfloat16),
        in_specs=[SMEM, VMEM, VMEM, VMEM, VMEM],
        out_specs=VMEM,
        scratch_shapes=[pltpu.VMEM((width, width), jnp.bfloat16)],
        compiler_params=limit,
        name="right",
    )(coupling_cols, near, far, left, z_row)


def solution(mesh):
    return jax.shard_map(
        on_device,
        mesh=mesh,
        in_specs=(
            P(("dom", "pan"), None, None, None),
            P(("dom", "pan"), None),
            P(("dom", "pan")),
            P(("dom", "pan"), None, None),
        ),
        out_specs=P(("dom", "pan"), None, None, None),
        check_vma=False,
    )
```

```python
import functools

import jax
import jax.numpy as jnp
from jax import lax
from jax.experimental import pallas as pl
from jax.experimental.pallas import tpu as pltpu
from jax.sharding import PartitionSpec as P

FAR_CHUNKS = (4, 3)
EDGE_SLOT = 4


def other_panel(panel, panels):
    there = panel + 2 * (panel % 2) - 1
    return there if 0 <= there < panels else panel


def slots_of(cols_ref, panel, panels, blocks, put):
    count = cols_ref.shape[1]
    edge = (panel == 0) | (panel == panels - 1)
    near_used = jnp.int32(0)
    far_used = jnp.where(edge, EDGE_SLOT, 0).astype(jnp.int32)
    for k in range(count):
        col = cols_ref[0, k]
        near = (lax.div(col, 2 * blocks) == lax.div(panel, 2)) & (near_used < count - 1)
        put(k, col, near, jnp.where(near, near_used, far_used))
        near_used = near_used + near.astype(jnp.int32)
        far_used = far_used + 1 - near.astype(jnp.int32)


def iotas(half):
    rows = lax.broadcasted_iota(jnp.int32, (half, half), 0)
    lanes = lax.broadcasted_iota(jnp.int32, (half, half), 1)
    return rows, lanes


def load_kernel(block, factors, own, z_row, sem, row_sem):
    copy = pltpu.make_async_copy(factors, own, sem)
    copy.start()
    row_copy = pltpu.make_async_copy(factors.at[block[0]], z_row, row_sem)
    row_copy.start()
    row_copy.wait()
    copy.wait()


def left_kernel(z_row, tiles, left):
    turned = z_row[...].astype(jnp.float32).T.astype(jnp.bfloat16)
    for k in range(tiles.shape[1]):
        left[k] = jnp.dot(turned, tiles[0, k], preferred_element_type=jnp.float32).astype(jnp.bfloat16)


def send_kernel(near_wanted, panels, firsts, cols, own, mate, *rest):
    outs, source = rest[:-1], rest[-1]
    blocks, width, _ = own.shape
    half = width // 2
    me = lax.axis_index("pan")
    there = me + 2 * lax.rem(me, 2) - 1
    asker = me if near_wanted else jnp.where((there < 0) | (there >= panels), me, there)
    total = source.shape[0] - 1
    for slot in range(total):
        source[slot] = jnp.int32(0)

    def put(k, col, near, slot):
        local = lax.rem(col, blocks) + jnp.where(lax.div(col, blocks) == me, 0, blocks)
        source[jnp.where(near == near_wanted, slot, total)] = local

    slots_of(cols, asker, panels, blocks, put)

    rows, lanes = iotas(half)
    line = lax.broadcasted_iota(jnp.int32, (16, half), 0)
    for out, first, last in zip(outs, firsts[:-1], firsts[1:]):
        found = jnp.zeros((16, half), jnp.float32)
        for slot in range(first, last):
            index = source[slot]
            mine = index < blocks
            block = jnp.where(mine, index, index - blocks)

            def part(rows_of, lanes_of):
                return jnp.where(mine, own[block, rows_of, lanes_of], mate[block, rows_of, lanes_of])

            head, tail = slice(0, half), slice(half, width)
            upper = part(head, head).astype(jnp.float32)
            lower = part(tail, tail).astype(jnp.float32)
            base = (slot - first) * width
            triangle = jnp.where(rows <= lanes, upper, lower.T)
            out[base : base + half, :] = triangle.astype(jnp.bfloat16)
            out[base + half : base + width, :] = part(head, tail)
            diagonal = jnp.sum(jnp.where(rows == lanes, lower, 0.0), axis=0, keepdims=True)
            found = jnp.where(line == slot - first, diagonal, found)
        out[(last - first) * width :, :] = found.astype(jnp.bfloat16)


def right_kernel(near_wanted, panels, blocks, first, cols, message, left, z_row, *rest):
    out, results, places, sems = rest[-4:]
    slots, width, _ = results.shape
    half = width // 2
    me = lax.axis_index("pan")
    for slot in range(slots):
        places[slot] = jnp.int32(-1)

    def put(k, col, near, slot):
        here = (near == near_wanted) & (slot >= first) & (slot < first + slots)
        places[jnp.where(here, slot - first, slots)] = jnp.int32(k)

    slots_of(cols, me, panels, blocks, put)

    rows, lanes = iotas(half)
    diagonals = message[slots * width :, :].astype(jnp.float32)
    for slot in range(slots):
        k = places[slot]
        base = slot * width
        triangle = message[base : base + half, :].astype(jnp.float32)
        upper = jnp.where(rows <= lanes, triangle, 0.0).astype(jnp.bfloat16)
        lower = jnp.where(rows < lanes, triangle.T, jnp.where(rows == lanes, diagonals[slot : slot + 1, :], 0.0))
        lower = lower.astype(jnp.bfloat16)
        corner = message[base + half : base + width, :]
        z_col = jnp.concatenate(
            [
                jnp.concatenate([upper, corner], axis=1),
                jnp.concatenate([jnp.zeros_like(lower), lower], axis=1),
            ],
            axis=0,
        )
        inner = jnp.dot(left[jnp.maximum(k, 0)], z_col, preferred_element_type=jnp.float32)
        product = jnp.dot(z_row[...], inner.astype(jnp.bfloat16), preferred_element_type=jnp.float32)
        results[slot] = (-0.5 * product).astype(jnp.bfloat16)

        @pl.when(k >= 0)
        def _():
            pltpu.make_async_copy(results.at[slot], out.at[0, k], sems.at[slot]).start()

    for slot in range(slots):

        @pl.when(places[slot] >= 0)
        def _():
            pltpu.make_async_copy(results.at[slot], out.at[0, 0], sems.at[slot]).wait()


VMEM = pl.BlockSpec(memory_space=pltpu.VMEM)
SMEM = pl.BlockSpec(memory_space=pltpu.SMEM)
HBM = pl.BlockSpec(memory_space=pltpu.HBM)


def on_device(coupling_tiles, coupling_cols, row_blocks, factor_tiles):
    doms, panels = lax.axis_size("dom"), lax.axis_size("pan")
    blocks, width, _ = factor_tiles.shape
    _, count, _, _ = coupling_tiles.shape
    half, slots = width // 2, count - 1
    limit = pltpu.CompilerParams(vmem_limit_bytes=32 * 2**20)
    bf16 = lambda *shape: jax.ShapeDtypeStruct(shape, jnp.bfloat16)

    def flat(dom, panel):
        return dom * panels + panel

    straight = [(dom, dom ^ (doms // 2)) for dom in range(doms)]
    ends = (0, panels - 1)

    def across(with_ends):
        return [
            (flat(dom, panel), flat(dom ^ (doms // 2), other_panel(panel, panels)))
            for dom in range(doms)
            for panel in range(panels)
            if with_ends or panel not in ends
        ]

    mate = lax.ppermute(factor_tiles, "pan", [(panel, panel ^ 1) for panel in range(panels)])
    near_cols = lax.ppermute(coupling_cols, "dom", straight)
    far_cols = lax.ppermute(coupling_cols, ("dom", "pan"), across(True))

    own, z_row = pl.pallas_call(
        load_kernel,
        out_shape=(bf16(blocks, width, width), bf16(width, width)),
        in_specs=[SMEM, HBM],
        out_specs=(VMEM,) * 2,
        scratch_shapes=[pltpu.SemaphoreType.DMA] * 2,
        compiler_params=limit,
        name="load",
    )(row_blocks, factor_tiles)

    def filled(near_wanted, sizes, cols):
        firsts = [sum(sizes[:i]) for i in range(len(sizes) + 1)]
        return pl.pallas_call(
            functools.partial(send_kernel, near_wanted, panels, firsts),
            out_shape=tuple(bf16(size * width + 16, half) for size in sizes),
            in_specs=[SMEM, VMEM, VMEM],
            out_specs=(VMEM,) * len(sizes),
            scratch_shapes=[pltpu.SMEM((slots + 1,), jnp.int32)],
            compiler_params=limit,
            name="fill_near" if near_wanted else "fill_far",
        )(cols, own, mate)

    (near,) = filled(True, (slots,), near_cols)
    near, far_cols = lax.optimization_barrier((near, far_cols))
    near = lax.ppermute(near, "dom", straight)
    far = filled(False, FAR_CHUNKS, far_cols)
    first = 0
    messages = [(True, 0, slots, near)]
    for size, message in zip(FAR_CHUNKS, far):
        with_ends = first <= EDGE_SLOT < first + size
        message = lax.ppermute(message, ("dom", "pan"), across(with_ends))
        messages.append((False, first, size, message))
        first += size

    left = pl.pallas_call(
        left_kernel,
        out_shape=bf16(count, width, width),
        in_specs=[VMEM, VMEM],
        out_specs=VMEM,
        compiler_params=limit,
        name="left",
    )(z_row, coupling_tiles)

    out = None
    for near_wanted, first, size, message in messages:
        out = pl.pallas_call(
            functools.partial(right_kernel, near_wanted, panels, blocks, first),
            out_shape=bf16(*coupling_tiles.shape),
            in_specs=[SMEM, VMEM, VMEM, VMEM] + ([] if out is None else [HBM]),
            out_specs=HBM,
            scratch_shapes=[
                pltpu.VMEM((size, width, width), jnp.bfloat16),
                pltpu.SMEM((size + 1,), jnp.int32),
                pltpu.SemaphoreType.DMA((size,)),
            ],
            input_output_aliases={} if out is None else {4: 0},
            compiler_params=limit,
            name="right_near" if near_wanted else "right_far",
        )(coupling_cols, message, left, z_row, *(() if out is None else (out,)))
    return out


def solution(mesh):
    return jax.shard_map(
        on_device,
        mesh=mesh,
        in_specs=(
            P(("dom", "pan"), None, None, None),
            P(("dom", "pan"), None),
            P(("dom", "pan")),
            P(("dom", "pan"), None, None),
        ),
        out_specs=P(("dom", "pan"), None, None, None),
        check_vma=False,
    )
```

```python
import functools

import jax
import jax.numpy as jnp
from jax import lax
from jax.experimental import pallas as pl
from jax.experimental.pallas import tpu as pltpu
from jax.sharding import PartitionSpec as P

NEAR, FAR, LAST = 5, 4, 3
IN_NEAR, IN_FAR, IN_LAST = range(3)


def other_panel(panel, panels):
    return panel + 2 * (panel % 2) - 1


def slots_of(cols_ref, panel, blocks, put):
    near_used = jnp.int32(0)
    far_used = jnp.int32(0)
    for k in range(cols_ref.shape[1]):
        col = cols_ref[0, k]
        near = lax.div(col, 2 * blocks) == lax.div(panel, 2)
        used = jnp.where(near, near_used, far_used)
        room = jnp.where(near, NEAR, FAR)
        direct = used < room
        message = jnp.where(direct, jnp.where(near, IN_NEAR, IN_FAR), IN_LAST)
        put(k, col, message, jnp.where(direct, used, used - room))
        near_used = near_used + near.astype(jnp.int32)
        far_used = far_used + 1 - near.astype(jnp.int32)


def iotas(half):
    rows = lax.broadcasted_iota(jnp.int32, (half, half), 0)
    lanes = lax.broadcasted_iota(jnp.int32, (half, half), 1)
    return rows, lanes


def load_kernel(block, factors, own, z_row, sem, row_sem):
    copy = pltpu.make_async_copy(factors, own, sem)
    copy.start()
    row_copy = pltpu.make_async_copy(factors.at[block[0]], z_row, row_sem)
    row_copy.start()
    row_copy.wait()
    copy.wait()


def left_kernel(z_row, tiles, left):
    turned = z_row[...].astype(jnp.float32).T.astype(jnp.bfloat16)
    for k in range(tiles.shape[1]):
        left[k] = jnp.dot(turned, tiles[0, k], preferred_element_type=jnp.float32).astype(jnp.bfloat16)


def write_slot(out, slot, found, tile_part, width):
    half = width // 2
    rows, lanes = iotas(half)
    line = lax.broadcasted_iota(jnp.int32, (16, half), 0)
    head, tail = slice(0, half), slice(half, width)
    upper = tile_part(head, head).astype(jnp.float32)
    lower = tile_part(tail, tail).astype(jnp.float32)
    base = slot * width
    out[base : base + half, :] = jnp.where(rows <= lanes, upper, lower.T).astype(jnp.bfloat16)
    out[base + half : base + width, :] = tile_part(head, tail)
    diagonal = jnp.sum(jnp.where(rows == lanes, lower, 0.0), axis=0, keepdims=True)
    return jnp.where(line == slot, diagonal, found)


def chosen(index, own, mate):
    blocks = own.shape[0]
    mine = index < blocks
    block = jnp.where(mine, index, jnp.where(index < 2 * blocks, index - blocks, 0))
    return lambda rows, lanes: jnp.where(mine, own[block, rows, lanes], mate[block, rows, lanes])


def near_kernel(cols, own, mate, out, source):
    blocks, width, _ = own.shape
    me = lax.axis_index("pan")
    for slot in range(NEAR):
        source[slot] = jnp.int32(0)

    def put(k, col, message, slot):
        local = lax.rem(col, blocks) + jnp.where(lax.div(col, blocks) == me, 0, blocks)
        source[jnp.where(message == IN_NEAR, slot, NEAR)] = local

    slots_of(cols, me, blocks, put)
    found = jnp.zeros((16, width // 2), jnp.float32)
    for slot in range(NEAR):
        found = write_slot(out, slot, found, chosen(source[slot], own, mate), width)
    out[NEAR * width :, :] = found.astype(jnp.bfloat16)


def far_kernel(cols, own, far_out, relay_out, source):
    blocks, width, _ = own.shape
    relayed = relay_out.shape[0] // width
    total = FAR + relayed
    me = lax.axis_index("pan")
    there = me + 2 * lax.rem(me, 2) - 1
    for slot in range(total):
        source[slot] = jnp.int32(0)

    def put(k, col, message, slot):
        far = lax.div(col, blocks) == me
        place = jnp.where(message == IN_FAR, slot, FAR + slot)
        source[jnp.where(far, jnp.minimum(place, total), total)] = lax.rem(col, blocks)

    slots_of(cols, there, blocks, put)
    for out, first, size in ((far_out, 0, FAR), (relay_out, FAR, relayed)):
        found = jnp.zeros((16, width // 2), jnp.float32)
        for slot in range(size):
            found = write_slot(out, slot, found, chosen(source[first + slot], own, own), width)
        out[size * width :, :] = found.astype(jnp.bfloat16)


def last_kernel(cols, own, mate, relay, out, source):
    blocks, width, _ = own.shape
    half = width // 2
    relayed = relay.shape[0] // width
    me = lax.axis_index("pan")
    for slot in range(LAST):
        source[slot] = jnp.int32(0)

    def put(k, col, message, slot):
        local = lax.rem(col, blocks) + jnp.where(lax.div(col, blocks) == me, 0, blocks)
        near = lax.div(col, 2 * blocks) == lax.div(me, 2)
        source[jnp.where(message == IN_LAST, slot, LAST)] = jnp.where(near, local, 2 * blocks)

    slots_of(cols, me, blocks, put)
    line = lax.broadcasted_iota(jnp.int32, (16, half), 0)
    found = jnp.zeros((16, half), jnp.float32)
    for slot in range(LAST):
        found = write_slot(out, slot, found, chosen(source[slot], own, mate), width)
    for slot in range(min(LAST, relayed)):
        base = slot * width
        theirs = source[slot] >= 2 * blocks
        out[base : base + width, :] = jnp.where(theirs, relay[base : base + width, :], out[base : base + width, :])
        found = jnp.where((line == slot) & theirs, relay[relayed * width :, :].astype(jnp.float32), found)
    out[LAST * width :, :] = found.astype(jnp.bfloat16)


def right_kernel(wanted, blocks, cols, received, left, z_row, *rest):
    out, results, places, sems = rest[-4:]
    slots, width, _ = results.shape
    half = width // 2
    me = lax.axis_index("pan")
    for slot in range(slots):
        places[slot] = jnp.int32(-1)

    def put(k, col, message, slot):
        places[jnp.where(message == wanted, slot, slots)] = jnp.int32(k)

    slots_of(cols, me, blocks, put)

    rows, lanes = iotas(half)
    diagonals = received[slots * width :, :].astype(jnp.float32)
    for slot in range(slots):
        k = places[slot]
        base = slot * width
        triangle = received[base : base + half, :].astype(jnp.float32)
        upper = jnp.where(rows <= lanes, triangle, 0.0).astype(jnp.bfloat16)
        lower = jnp.where(rows < lanes, triangle.T, jnp.where(rows == lanes, diagonals[slot : slot + 1, :], 0.0))
        lower = lower.astype(jnp.bfloat16)
        corner = received[base + half : base + width, :]
        z_col = jnp.concatenate(
            [
                jnp.concatenate([upper, corner], axis=1),
                jnp.concatenate([jnp.zeros_like(lower), lower], axis=1),
            ],
            axis=0,
        )
        inner = jnp.dot(left[jnp.maximum(k, 0)], z_col, preferred_element_type=jnp.float32)
        product = jnp.dot(z_row[...], inner.astype(jnp.bfloat16), preferred_element_type=jnp.float32)
        results[slot] = (-0.5 * product).astype(jnp.bfloat16)

    for slot in range(slots):
        k = places[slot]

        @pl.when(k >= 0)
        def _():
            pltpu.make_async_copy(results.at[slot], out.at[0, k], sems.at[slot]).start()

    for slot in range(slots):

        @pl.when(places[slot] >= 0)
        def _():
            pltpu.make_async_copy(results.at[slot], out.at[0, 0], sems.at[slot]).wait()


RIGHT_COST = (2 * 10**9,) * 3
LEFT_COST = 1
TINY = pl.CostEstimate(flops=1, bytes_accessed=1, transcendentals=0)
VMEM = pl.BlockSpec(memory_space=pltpu.VMEM)
SMEM = pl.BlockSpec(memory_space=pltpu.SMEM)
HBM = pl.BlockSpec(memory_space=pltpu.HBM)


def on_device(coupling_tiles, coupling_cols, row_blocks, factor_tiles):
    doms, panels = lax.axis_size("dom"), lax.axis_size("pan")
    blocks, width, _ = factor_tiles.shape
    _, count, _, _ = coupling_tiles.shape
    half, slots = width // 2, count - 1
    limit = pltpu.CompilerParams(vmem_limit_bytes=32 * 2**20)
    bf16 = lambda *shape: jax.ShapeDtypeStruct(shape, jnp.bfloat16)

    def flat(dom, panel):
        return dom * panels + panel

    straight = [(dom, dom ^ (doms // 2)) for dom in range(doms)]
    ends = (0, panels - 1)

    across = [
        (flat(dom, panel), flat(dom ^ (doms // 2), other_panel(panel, panels)))
        for dom in range(doms)
        for panel in range(panels)
        if panel not in ends
    ]
    beside = [
        (flat(dom, panel), flat(dom, other_panel(panel, panels)))
        for dom in range(doms)
        for panel in range(panels)
        if panel not in ends
    ]

    far_cols = lax.ppermute(coupling_cols, ("dom", "pan"), across)
    near_cols = lax.ppermute(coupling_cols, "dom", straight)

    own, z_row = pl.pallas_call(
        load_kernel,
        out_shape=(bf16(blocks, width, width), bf16(width, width)),
        in_specs=[SMEM, HBM],
        out_specs=(VMEM,) * 2,
        scratch_shapes=[pltpu.SemaphoreType.DMA] * 2,
        compiler_params=limit,
        cost_estimate=TINY,
        name="load",
    )(row_blocks, factor_tiles)

    def fill(kernel, sizes, *operands):
        return pl.pallas_call(
            kernel,
            out_shape=tuple(bf16(size * width + 16, half) for size in sizes),
            in_specs=[SMEM] + [VMEM] * (len(operands) - 1),
            out_specs=(VMEM,) * len(sizes),
            scratch_shapes=[pltpu.SMEM((sum(sizes) + 1,), jnp.int32)],
            compiler_params=limit,
            cost_estimate=TINY,
            name=kernel.__name__,
        )(*operands)

    far, relay = fill(far_kernel, (FAR, slots - FAR), far_cols, own)
    far, relay, near_cols, given = lax.optimization_barrier((far, relay, near_cols, factor_tiles))
    far = lax.ppermute(far, ("dom", "pan"), across)
    mate = lax.ppermute(given, "pan", [(panel, panel ^ 1) for panel in range(panels)])
    relay = lax.ppermute(relay, ("dom", "pan"), beside)
    (near,) = fill(near_kernel, (NEAR,), near_cols, own, mate)
    near = lax.ppermute(near, "dom", straight)
    (last,) = fill(last_kernel, (LAST,), near_cols, own, mate, relay)
    last = lax.ppermute(last, "dom", straight)
    messages = [(IN_FAR, FAR, far), (IN_NEAR, NEAR, near), (IN_LAST, LAST, last)]

    left = pl.pallas_call(
        left_kernel,
        out_shape=bf16(count, width, width),
        in_specs=[VMEM, VMEM],
        out_specs=VMEM,
        compiler_params=limit,
        cost_estimate=pl.CostEstimate(flops=LEFT_COST, bytes_accessed=1, transcendentals=0),
        name="left",
    )(z_row, coupling_tiles)

    out = None
    for wanted, size, message in messages:
        out = pl.pallas_call(
            functools.partial(right_kernel, wanted, blocks),
            out_shape=bf16(*coupling_tiles.shape),
            in_specs=[SMEM, VMEM, VMEM, VMEM] + ([] if out is None else [HBM]),
            out_specs=HBM,
            scratch_shapes=[
                pltpu.VMEM((size, width, width), jnp.bfloat16),
                pltpu.SMEM((size + 1,), jnp.int32),
                pltpu.SemaphoreType.DMA((size,)),
            ],
            input_output_aliases={} if out is None else {4: 0},
            compiler_params=limit,
            cost_estimate=pl.CostEstimate(flops=RIGHT_COST[wanted], bytes_accessed=1, transcendentals=0),
            name=("right_near", "right_far", "right_last")[wanted],
        )(coupling_cols, message, left, z_row, *(() if out is None else (out,)))
    return out


def solution(mesh):
    return jax.shard_map(
        on_device,
        mesh=mesh,
        in_specs=(
            P(("dom", "pan"), None, None, None),
            P(("dom", "pan"), None),
            P(("dom", "pan")),
            P(("dom", "pan"), None, None),
        ),
        out_specs=P(("dom", "pan"), None, None, None),
        check_vma=False,
    )
```

```python
import functools

import jax
import jax.numpy as jnp
from jax import lax
from jax.experimental import pallas as pl
from jax.experimental.pallas import tpu as pltpu
from jax.sharding import PartitionSpec as P

FAR_CHUNKS = (4, 3)
EDGE_SLOT = 4


def other_panel(panel, panels):
    there = panel + 2 * (panel % 2) - 1
    return there if 0 <= there < panels else panel


def slots_of(cols_ref, panel, panels, blocks, put):
    count = cols_ref.shape[1]
    edge = (panel == 0) | (panel == panels - 1)
    near_used = jnp.int32(0)
    far_used = jnp.where(edge, EDGE_SLOT, 0).astype(jnp.int32)
    for k in range(count):
        col = cols_ref[0, k]
        near = (lax.div(col, 2 * blocks) == lax.div(panel, 2)) & (near_used < count - 1)
        put(k, col, near, jnp.where(near, near_used, far_used))
        near_used = near_used + near.astype(jnp.int32)
        far_used = far_used + 1 - near.astype(jnp.int32)


def iotas(half):
    rows = lax.broadcasted_iota(jnp.int32, (half, half), 0)
    lanes = lax.broadcasted_iota(jnp.int32, (half, half), 1)
    return rows, lanes


def load_kernel(block, factors, own, z_row, sem, row_sem):
    copy = pltpu.make_async_copy(factors, own, sem)
    copy.start()
    row_copy = pltpu.make_async_copy(factors.at[block[0]], z_row, row_sem)
    row_copy.start()
    row_copy.wait()
    copy.wait()


def left_kernel(z_row, tiles, left):
    turned = z_row[...].astype(jnp.float32).T.astype(jnp.bfloat16)
    for k in range(tiles.shape[1]):
        left[k] = jnp.dot(turned, tiles[0, k], preferred_element_type=jnp.float32).astype(jnp.bfloat16)


def send_kernel(near_wanted, panels, firsts, cols, own, mate, *rest):
    outs, source = rest[:-1], rest[-1]
    blocks, width, _ = own.shape
    half = width // 2
    me = lax.axis_index("pan")
    there = me + 2 * lax.rem(me, 2) - 1
    asker = me if near_wanted else jnp.where((there < 0) | (there >= panels), me, there)
    total = source.shape[0] - 1
    for slot in range(total):
        source[slot] = jnp.int32(0)

    def put(k, col, near, slot):
        local = lax.rem(col, blocks) + jnp.where(lax.div(col, blocks) == me, 0, blocks)
        source[jnp.where(near == near_wanted, slot, total)] = local

    slots_of(cols, asker, panels, blocks, put)

    rows, lanes = iotas(half)
    line = lax.broadcasted_iota(jnp.int32, (16, half), 0)
    for out, first, last in zip(outs, firsts[:-1], firsts[1:]):
        found = jnp.zeros((16, half), jnp.float32)
        for slot in range(first, last):
            index = source[slot]
            mine = index < blocks
            block = jnp.where(mine, index, index - blocks)

            def part(rows_of, lanes_of):
                return jnp.where(mine, own[block, rows_of, lanes_of], mate[block, rows_of, lanes_of])

            head, tail = slice(0, half), slice(half, width)
            upper = part(head, head).astype(jnp.float32)
            lower = part(tail, tail).astype(jnp.float32)
            base = (slot - first) * width
            triangle = jnp.where(rows <= lanes, upper, lower.T)
            out[base : base + half, :] = triangle.astype(jnp.bfloat16)
            out[base + half : base + width, :] = part(head, tail)
            diagonal = jnp.sum(jnp.where(rows == lanes, lower, 0.0), axis=0, keepdims=True)
            found = jnp.where(line == slot - first, diagonal, found)
        out[(last - first) * width :, :] = found.astype(jnp.bfloat16)


def right_kernel(near_wanted, panels, blocks, first, cols, message, left, z_row, *rest):
    out, results, places, sems = rest[-4:]
    slots, width, _ = results.shape
    half = width // 2
    me = lax.axis_index("pan")
    for slot in range(slots):
        places[slot] = jnp.int32(-1)

    def put(k, col, near, slot):
        here = (near == near_wanted) & (slot >= first) & (slot < first + slots)
        places[jnp.where(here, slot - first, slots)] = jnp.int32(k)

    slots_of(cols, me, panels, blocks, put)

    rows, lanes = iotas(half)
    diagonals = message[slots * width :, :].astype(jnp.float32)
    for slot in range(slots):
        k = places[slot]
        base = slot * width
        triangle = message[base : base + half, :].astype(jnp.float32)
        upper = jnp.where(rows <= lanes, triangle, 0.0).astype(jnp.bfloat16)
        lower = jnp.where(rows < lanes, triangle.T, jnp.where(rows == lanes, diagonals[slot : slot + 1, :], 0.0))
        lower = lower.astype(jnp.bfloat16)
        corner = message[base + half : base + width, :]
        z_col = jnp.concatenate(
            [
                jnp.concatenate([upper, corner], axis=1),
                jnp.concatenate([jnp.zeros_like(lower), lower], axis=1),
            ],
            axis=0,
        )
        inner = jnp.dot(left[jnp.maximum(k, 0)], z_col, preferred_element_type=jnp.float32)
        product = jnp.dot(z_row[...], inner.astype(jnp.bfloat16), preferred_element_type=jnp.float32)
        results[slot] = (-0.5 * product).astype(jnp.bfloat16)

    for slot in range(slots):
        k = places[slot]

        @pl.when(k >= 0)
        def _():
            pltpu.make_async_copy(results.at[slot], out.at[0, k], sems.at[slot]).start()

    for slot in range(slots):

        @pl.when(places[slot] >= 0)
        def _():
            pltpu.make_async_copy(results.at[slot], out.at[0, 0], sems.at[slot]).wait()


RIGHT_COST = 1
TINY = pl.CostEstimate(flops=1, bytes_accessed=1, transcendentals=0)
COST = pl.CostEstimate(flops=RIGHT_COST, bytes_accessed=1, transcendentals=0)
VMEM = pl.BlockSpec(memory_space=pltpu.VMEM)
SMEM = pl.BlockSpec(memory_space=pltpu.SMEM)
HBM = pl.BlockSpec(memory_space=pltpu.HBM)


def on_device(coupling_tiles, coupling_cols, row_blocks, factor_tiles):
    doms, panels = lax.axis_size("dom"), lax.axis_size("pan")
    blocks, width, _ = factor_tiles.shape
    _, count, _, _ = coupling_tiles.shape
    half, slots = width // 2, count - 1
    limit = pltpu.CompilerParams(vmem_limit_bytes=32 * 2**20)
    bf16 = lambda *shape: jax.ShapeDtypeStruct(shape, jnp.bfloat16)

    def flat(dom, panel):
        return dom * panels + panel

    straight = [(dom, dom ^ (doms // 2)) for dom in range(doms)]
    ends = (0, panels - 1)

    def across(with_ends):
        return [
            (flat(dom, panel), flat(dom ^ (doms // 2), other_panel(panel, panels)))
            for dom in range(doms)
            for panel in range(panels)
            if with_ends or panel not in ends
        ]

    mate = lax.ppermute(factor_tiles, "pan", [(panel, panel ^ 1) for panel in range(panels)])
    near_cols = lax.ppermute(coupling_cols, "dom", straight)
    far_cols = lax.ppermute(coupling_cols, ("dom", "pan"), across(True))

    own, z_row = pl.pallas_call(
        load_kernel,
        out_shape=(bf16(blocks, width, width), bf16(width, width)),
        in_specs=[SMEM, HBM],
        out_specs=(VMEM,) * 2,
        scratch_shapes=[pltpu.SemaphoreType.DMA] * 2,
        compiler_params=limit,
        cost_estimate=TINY,
        name="load",
    )(row_blocks, factor_tiles)

    def filled(near_wanted, sizes, cols):
        firsts = [sum(sizes[:i]) for i in range(len(sizes) + 1)]
        return pl.pallas_call(
            functools.partial(send_kernel, near_wanted, panels, firsts),
            out_shape=tuple(bf16(size * width + 16, half) for size in sizes),
            in_specs=[SMEM, VMEM, VMEM],
            out_specs=(VMEM,) * len(sizes),
            scratch_shapes=[pltpu.SMEM((slots + 1,), jnp.int32)],
            compiler_params=limit,
            cost_estimate=TINY,
            name="fill_near" if near_wanted else "fill_far",
        )(cols, own, mate)

    (near,) = filled(True, (slots,), near_cols)
    near = lax.ppermute(near, "dom", straight)
    far = filled(False, FAR_CHUNKS, far_cols)
    first = 0
    messages = [(True, 0, slots, near)]
    for size, message in zip(FAR_CHUNKS, far):
        with_ends = first <= EDGE_SLOT < first + size
        message = lax.ppermute(message, ("dom", "pan"), across(with_ends))
        messages.append((False, first, size, message))
        first += size

    left = pl.pallas_call(
        left_kernel,
        out_shape=bf16(count, width, width),
        in_specs=[VMEM, VMEM],
        out_specs=VMEM,
        compiler_params=limit,
        cost_estimate=TINY,
        name="left",
    )(z_row, coupling_tiles)

    out = None
    for near_wanted, first, size, message in messages:
        out = pl.pallas_call(
            functools.partial(right_kernel, near_wanted, panels, blocks, first),
            out_shape=bf16(*coupling_tiles.shape),
            in_specs=[SMEM, VMEM, VMEM, VMEM] + ([] if out is None else [HBM]),
            out_specs=HBM,
            scratch_shapes=[
                pltpu.VMEM((size, width, width), jnp.bfloat16),
                pltpu.SMEM((size + 1,), jnp.int32),
                pltpu.SemaphoreType.DMA((size,)),
            ],
            input_output_aliases={} if out is None else {4: 0},
            compiler_params=limit,
            cost_estimate=COST,
            name="right_near" if near_wanted else "right_far",
        )(coupling_cols, message, left, z_row, *(() if out is None else (out,)))
    return out


def solution(mesh):
    return jax.shard_map(
        on_device,
        mesh=mesh,
        in_specs=(
            P(("dom", "pan"), None, None, None),
            P(("dom", "pan"), None),
            P(("dom", "pan")),
            P(("dom", "pan"), None, None),
        ),
        out_specs=P(("dom", "pan"), None, None, None),
        check_vma=False,
    )
```

```python
import functools

import jax
import jax.numpy as jnp
from jax import lax
from jax.experimental import pallas as pl
from jax.experimental.pallas import tpu as pltpu
from jax.sharding import PartitionSpec as P

NEAR, FAR, LAST = 5, 5, 3
IN_NEAR, IN_FAR, IN_LAST = range(3)


def other_panel(panel, panels):
    return panel + 2 * (panel % 2) - 1


def slots_of(cols_ref, panel, blocks, put):
    near_used = jnp.int32(0)
    far_used = jnp.int32(0)
    for k in range(cols_ref.shape[1]):
        col = cols_ref[0, k]
        near = lax.div(col, 2 * blocks) == lax.div(panel, 2)
        used = jnp.where(near, near_used, far_used)
        room = jnp.where(near, NEAR, FAR)
        direct = used < room
        message = jnp.where(direct, jnp.where(near, IN_NEAR, IN_FAR), IN_LAST)
        put(k, col, message, jnp.where(direct, used, used - room))
        near_used = near_used + near.astype(jnp.int32)
        far_used = far_used + 1 - near.astype(jnp.int32)


def iotas(half):
    rows = lax.broadcasted_iota(jnp.int32, (half, half), 0)
    lanes = lax.broadcasted_iota(jnp.int32, (half, half), 1)
    return rows, lanes


def load_kernel(block, factors, own, z_row, sem, row_sem):
    copy = pltpu.make_async_copy(factors, own, sem)
    copy.start()
    row_copy = pltpu.make_async_copy(factors.at[block[0]], z_row, row_sem)
    row_copy.start()
    row_copy.wait()
    copy.wait()


def left_kernel(z_row, tiles, left):
    turned = z_row[...].astype(jnp.float32).T.astype(jnp.bfloat16)
    for k in range(tiles.shape[1]):
        left[k] = jnp.dot(turned, tiles[0, k], preferred_element_type=jnp.float32).astype(jnp.bfloat16)


def write_slot(out, slot, found, tile_part, width):
    half = width // 2
    rows, lanes = iotas(half)
    line = lax.broadcasted_iota(jnp.int32, (16, half), 0)
    head, tail = slice(0, half), slice(half, width)
    upper = tile_part(head, head).astype(jnp.float32)
    lower = tile_part(tail, tail).astype(jnp.float32)
    base = slot * width
    out[base : base + half, :] = jnp.where(rows <= lanes, upper, lower.T).astype(jnp.bfloat16)
    out[base + half : base + width, :] = tile_part(head, tail)
    diagonal = jnp.sum(jnp.where(rows == lanes, lower, 0.0), axis=0, keepdims=True)
    return jnp.where(line == slot, diagonal, found)


def chosen(index, own, mate):
    blocks = own.shape[0]
    mine = index < blocks
    block = jnp.where(mine, index, jnp.where(index < 2 * blocks, index - blocks, 0))
    return lambda rows, lanes: jnp.where(mine, own[block, rows, lanes], mate[block, rows, lanes])


def near_kernel(cols, own, mate, out, source):
    blocks, width, _ = own.shape
    me = lax.axis_index("pan")
    for slot in range(NEAR):
        source[slot] = jnp.int32(0)

    def put(k, col, message, slot):
        local = lax.rem(col, blocks) + jnp.where(lax.div(col, blocks) == me, 0, blocks)
        source[jnp.where(message == IN_NEAR, slot, NEAR)] = local

    slots_of(cols, me, blocks, put)
    found = jnp.zeros((16, width // 2), jnp.float32)
    for slot in range(NEAR):
        found = write_slot(out, slot, found, chosen(source[slot], own, mate), width)
    out[NEAR * width :, :] = found.astype(jnp.bfloat16)


def far_kernel(cols, own, far_out, relay_out, source):
    blocks, width, _ = own.shape
    relayed = relay_out.shape[0] // width
    total = FAR + relayed
    me = lax.axis_index("pan")
    there = me + 2 * lax.rem(me, 2) - 1
    for slot in range(total):
        source[slot] = jnp.int32(0)

    def put(k, col, message, slot):
        far = lax.div(col, blocks) == me
        place = jnp.where(message == IN_FAR, slot, FAR + slot)
        source[jnp.where(far, jnp.minimum(place, total), total)] = lax.rem(col, blocks)

    slots_of(cols, there, blocks, put)
    for out, first, size in ((far_out, 0, FAR), (relay_out, FAR, relayed)):
        found = jnp.zeros((16, width // 2), jnp.float32)
        for slot in range(size):
            found = write_slot(out, slot, found, chosen(source[first + slot], own, own), width)
        out[size * width :, :] = found.astype(jnp.bfloat16)


def last_kernel(cols, own, mate, relay, out, source):
    blocks, width, _ = own.shape
    half = width // 2
    relayed = relay.shape[0] // width
    me = lax.axis_index("pan")
    for slot in range(LAST):
        source[slot] = jnp.int32(0)

    def put(k, col, message, slot):
        local = lax.rem(col, blocks) + jnp.where(lax.div(col, blocks) == me, 0, blocks)
        near = lax.div(col, 2 * blocks) == lax.div(me, 2)
        source[jnp.where(message == IN_LAST, slot, LAST)] = jnp.where(near, local, 2 * blocks)

    slots_of(cols, me, blocks, put)
    line = lax.broadcasted_iota(jnp.int32, (16, half), 0)
    found = jnp.zeros((16, half), jnp.float32)
    for slot in range(LAST):
        found = write_slot(out, slot, found, chosen(source[slot], own, mate), width)
    for slot in range(min(LAST, relayed)):
        base = slot * width
        theirs = source[slot] >= 2 * blocks
        out[base : base + width, :] = jnp.where(theirs, relay[base : base + width, :], out[base : base + width, :])
        found = jnp.where((line == slot) & theirs, relay[relayed * width :, :].astype(jnp.float32), found)
    out[LAST * width :, :] = found.astype(jnp.bfloat16)


def right_kernel(wanted, blocks, cols, received, left, z_row, *rest):
    out, results, places, sems = rest[-4:]
    slots, width, _ = results.shape
    half = width // 2
    me = lax.axis_index("pan")
    for slot in range(slots):
        places[slot] = jnp.int32(-1)

    def put(k, col, message, slot):
        places[jnp.where(message == wanted, slot, slots)] = jnp.int32(k)

    slots_of(cols, me, blocks, put)

    rows, lanes = iotas(half)
    diagonals = received[slots * width :, :].astype(jnp.float32)
    for slot in range(slots):
        k = places[slot]
        base = slot * width
        triangle = received[base : base + half, :].astype(jnp.float32)
        upper = jnp.where(rows <= lanes, triangle, 0.0).astype(jnp.bfloat16)
        lower = jnp.where(rows < lanes, triangle.T, jnp.where(rows == lanes, diagonals[slot : slot + 1, :], 0.0))
        lower = lower.astype(jnp.bfloat16)
        corner = received[base + half : base + width, :]
        z_col = jnp.concatenate(
            [
                jnp.concatenate([upper, corner], axis=1),
                jnp.concatenate([jnp.zeros_like(lower), lower], axis=1),
            ],
            axis=0,
        )
        inner = jnp.dot(left[jnp.maximum(k, 0)], z_col, preferred_element_type=jnp.float32)
        product = jnp.dot(z_row[...], inner.astype(jnp.bfloat16), preferred_element_type=jnp.float32)
        results[slot] = (-0.5 * product).astype(jnp.bfloat16)

    for slot in range(slots):
        k = places[slot]

        @pl.when(k >= 0)
        def _():
            pltpu.make_async_copy(results.at[slot], out.at[0, k], sems.at[slot]).start()

    for slot in range(slots):

        @pl.when(places[slot] >= 0)
        def _():
            pltpu.make_async_copy(results.at[slot], out.at[0, 0], sems.at[slot]).wait()


RIGHT_COST = (4*10**9,) * 3
LEFT_COST = 1
TINY = pl.CostEstimate(flops=1, bytes_accessed=1, transcendentals=0)
VMEM = pl.BlockSpec(memory_space=pltpu.VMEM)
SMEM = pl.BlockSpec(memory_space=pltpu.SMEM)
HBM = pl.BlockSpec(memory_space=pltpu.HBM)


def on_device(coupling_tiles, coupling_cols, row_blocks, factor_tiles):
    doms, panels = lax.axis_size("dom"), lax.axis_size("pan")
    blocks, width, _ = factor_tiles.shape
    _, count, _, _ = coupling_tiles.shape
    half, slots = width // 2, count - 1
    limit = pltpu.CompilerParams(vmem_limit_bytes=32 * 2**20)
    bf16 = lambda *shape: jax.ShapeDtypeStruct(shape, jnp.bfloat16)

    def flat(dom, panel):
        return dom * panels + panel

    straight = [(dom, dom ^ (doms // 2)) for dom in range(doms)]
    ends = (0, panels - 1)

    across = [
        (flat(dom, panel), flat(dom ^ (doms // 2), other_panel(panel, panels)))
        for dom in range(doms)
        for panel in range(panels)
        if panel not in ends
    ]
    beside = [
        (flat(dom, panel), flat(dom, other_panel(panel, panels)))
        for dom in range(doms)
        for panel in range(panels)
        if panel not in ends
    ]

    far_cols = lax.ppermute(coupling_cols, ("dom", "pan"), across)

    own, z_row = pl.pallas_call(
        load_kernel,
        out_shape=(bf16(blocks, width, width), bf16(width, width)),
        in_specs=[SMEM, HBM],
        out_specs=(VMEM,) * 2,
        scratch_shapes=[pltpu.SemaphoreType.DMA] * 2,
        compiler_params=limit,
        cost_estimate=TINY,
        name="load",
    )(row_blocks, factor_tiles)

    def fill(kernel, sizes, *operands):
        return pl.pallas_call(
            kernel,
            out_shape=tuple(bf16(size * width + 16, half) for size in sizes),
            in_specs=[SMEM] + [VMEM] * (len(operands) - 1),
            out_specs=(VMEM,) * len(sizes),
            scratch_shapes=[pltpu.SMEM((sum(sizes) + 1,), jnp.int32)],
            compiler_params=limit,
            cost_estimate=TINY,
            name=kernel.__name__,
        )(*operands)

    far, relay = fill(far_kernel, (FAR, slots - FAR), far_cols, own)
    far, relay, given, cols = lax.optimization_barrier((far, relay, factor_tiles, coupling_cols))
    far = lax.ppermute(far, ("dom", "pan"), across)
    mate = lax.ppermute(given, "pan", [(panel, panel ^ 1) for panel in range(panels)])
    near_cols = lax.ppermute(cols, "dom", straight)
    relay = lax.ppermute(relay, ("dom", "pan"), beside)
    (near,) = fill(near_kernel, (NEAR,), near_cols, own, mate)
    near = lax.ppermute(near, "dom", straight)
    (last,) = fill(last_kernel, (LAST,), near_cols, own, mate, relay)
    last = lax.ppermute(last, "dom", straight)
    messages = [(IN_FAR, FAR, far), (IN_NEAR, NEAR, near), (IN_LAST, LAST, last)]

    left = pl.pallas_call(
        left_kernel,
        out_shape=bf16(count, width, width),
        in_specs=[VMEM, VMEM],
        out_specs=VMEM,
        compiler_params=limit,
        cost_estimate=pl.CostEstimate(flops=LEFT_COST, bytes_accessed=1, transcendentals=0),
        name="left",
    )(z_row, coupling_tiles)

    out = None
    for wanted, size, message in messages:
        out = pl.pallas_call(
            functools.partial(right_kernel, wanted, blocks),
            out_shape=bf16(*coupling_tiles.shape),
            in_specs=[SMEM, VMEM, VMEM, VMEM] + ([] if out is None else [HBM]),
            out_specs=HBM,
            scratch_shapes=[
                pltpu.VMEM((size, width, width), jnp.bfloat16),
                pltpu.SMEM((size + 1,), jnp.int32),
                pltpu.SemaphoreType.DMA((size,)),
            ],
            input_output_aliases={} if out is None else {4: 0},
            compiler_params=limit,
            cost_estimate=pl.CostEstimate(flops=RIGHT_COST[wanted], bytes_accessed=1, transcendentals=0),
            name=("right_near", "right_far", "right_last")[wanted],
        )(coupling_cols, message, left, z_row, *(() if out is None else (out,)))
    return out


def solution(mesh):
    return jax.shard_map(
        on_device,
        mesh=mesh,
        in_specs=(
            P(("dom", "pan"), None, None, None),
            P(("dom", "pan"), None),
            P(("dom", "pan")),
            P(("dom", "pan"), None, None),
        ),
        out_specs=P(("dom", "pan"), None, None, None),
        check_vma=False,
    )
```

```python
import functools

import jax
import jax.numpy as jnp
from jax import lax
from jax.experimental import pallas as pl
from jax.experimental.pallas import tpu as pltpu
from jax.sharding import PartitionSpec as P

NEAR, FAR, LAST = 5, 5, 2
IN_NEAR, IN_FAR, IN_LAST, IN_EXTRA = range(4)


def other_panel(panel, panels):
    return panel + 2 * (panel % 2) - 1


def slots_of(cols_ref, panel, blocks, put):
    near_used = jnp.int32(0)
    far_used = jnp.int32(0)
    for k in range(cols_ref.shape[1]):
        col = cols_ref[0, k]
        near = lax.div(col, 2 * blocks) == lax.div(panel, 2)
        used = jnp.where(near, near_used, far_used)
        room = jnp.where(near, NEAR, FAR)
        direct = used < room
        over = used - room
        message = jnp.where(direct, jnp.where(near, IN_NEAR, IN_FAR), jnp.where(over < LAST, IN_LAST, IN_EXTRA))
        put(k, col, message, jnp.where(direct, used, jnp.where(over < LAST, over, 0)))
        near_used = near_used + near.astype(jnp.int32)
        far_used = far_used + 1 - near.astype(jnp.int32)


def iotas(half):
    rows = lax.broadcasted_iota(jnp.int32, (half, half), 0)
    lanes = lax.broadcasted_iota(jnp.int32, (half, half), 1)
    return rows, lanes


def load_kernel(block, factors, own, z_row, sem, row_sem):
    copy = pltpu.make_async_copy(factors, own, sem)
    copy.start()
    row_copy = pltpu.make_async_copy(factors.at[block[0]], z_row, row_sem)
    row_copy.start()
    row_copy.wait()
    copy.wait()


def left_kernel(z_row, tiles, left):
    turned = z_row[...].astype(jnp.float32).T.astype(jnp.bfloat16)
    for k in range(tiles.shape[1]):
        left[k] = jnp.dot(turned, tiles[0, k], preferred_element_type=jnp.float32).astype(jnp.bfloat16)


def write_slot(out, slot, found, tile_part, width):
    half = width // 2
    rows, lanes = iotas(half)
    line = lax.broadcasted_iota(jnp.int32, (16, half), 0)
    head, tail = slice(0, half), slice(half, width)
    upper = tile_part(head, head).astype(jnp.float32)
    lower = tile_part(tail, tail).astype(jnp.float32)
    base = slot * width
    out[base : base + half, :] = jnp.where(rows <= lanes, upper, lower.T).astype(jnp.bfloat16)
    out[base + half : base + width, :] = tile_part(head, tail)
    diagonal = jnp.sum(jnp.where(rows == lanes, lower, 0.0), axis=0, keepdims=True)
    return jnp.where(line == slot, diagonal, found)


def chosen(index, own, mate):
    blocks = own.shape[0]
    mine = index < blocks
    block = jnp.where(mine, index, jnp.where(index < 2 * blocks, index - blocks, 0))
    return lambda rows, lanes: jnp.where(mine, own[block, rows, lanes], mate[block, rows, lanes])


def near_kernel(cols, own, mate, out, source):
    blocks, width, _ = own.shape
    me = lax.axis_index("pan")
    for slot in range(NEAR):
        source[slot] = jnp.int32(0)

    def put(k, col, message, slot):
        local = lax.rem(col, blocks) + jnp.where(lax.div(col, blocks) == me, 0, blocks)
        source[jnp.where(message == IN_NEAR, slot, NEAR)] = local

    slots_of(cols, me, blocks, put)
    found = jnp.zeros((16, width // 2), jnp.float32)
    for slot in range(NEAR):
        found = write_slot(out, slot, found, chosen(source[slot], own, mate), width)
    out[NEAR * width :, :] = found.astype(jnp.bfloat16)


def far_kernel(cols, own, far_out, relay_out, source):
    blocks, width, _ = own.shape
    relayed = relay_out.shape[0] // width
    total = FAR + relayed
    me = lax.axis_index("pan")
    there = me + 2 * lax.rem(me, 2) - 1
    for slot in range(total):
        source[slot] = jnp.int32(0)

    def put(k, col, message, slot):
        far = lax.div(col, blocks) == me
        place = jnp.where(message == IN_FAR, slot, FAR + slot)
        source[jnp.where(far, jnp.minimum(place, total), total)] = lax.rem(col, blocks)

    slots_of(cols, there, blocks, put)
    for out, first, size in ((far_out, 0, FAR), (relay_out, FAR, relayed)):
        found = jnp.zeros((16, width // 2), jnp.float32)
        for slot in range(size):
            found = write_slot(out, slot, found, chosen(source[first + slot], own, own), width)
        out[size * width :, :] = found.astype(jnp.bfloat16)


def last_kernel(cols, own, mate, relay, out, extra_out, source):
    blocks, width, _ = own.shape
    half = width // 2
    relayed = relay.shape[0] // width
    me = lax.axis_index("pan")
    for slot in range(LAST + 1):
        source[slot] = jnp.int32(0)

    def put(k, col, message, slot):
        local = lax.rem(col, blocks) + jnp.where(lax.div(col, blocks) == me, 0, blocks)
        near = lax.div(col, 2 * blocks) == lax.div(me, 2)
        place = jnp.where(message == IN_LAST, slot, jnp.where(message == IN_EXTRA, LAST, LAST + 1))
        source[place] = jnp.where(near, local, 2 * blocks)

    slots_of(cols, me, blocks, put)
    line = lax.broadcasted_iota(jnp.int32, (16, half), 0)
    found = jnp.zeros((16, half), jnp.float32)
    for slot in range(LAST):
        found = write_slot(out, slot, found, chosen(source[slot], own, mate), width)
    for slot in range(min(LAST, relayed)):
        base = slot * width
        theirs = source[slot] >= 2 * blocks
        out[base : base + width, :] = jnp.where(theirs, relay[base : base + width, :], out[base : base + width, :])
        found = jnp.where((line == slot) & theirs, relay[relayed * width :, :].astype(jnp.float32), found)
    out[LAST * width :, :] = found.astype(jnp.bfloat16)
    found = jnp.zeros((16, half), jnp.float32)
    found = write_slot(extra_out, 0, found, chosen(source[LAST], own, mate), width)
    extra_out[width:, :] = found.astype(jnp.bfloat16)


def right_kernel(wanted, sizes, blocks, cols, left, z_row, *rest):
    received = rest[: len(wanted)]
    out, results, places, sems = rest[-4:]
    slots, width, _ = results.shape
    half = width // 2
    me = lax.axis_index("pan")
    for slot in range(slots):
        places[slot] = jnp.int32(-1)

    def put(k, col, message, slot):
        place = jnp.int32(slots)
        for i, kind in enumerate(wanted):
            place = jnp.where(message == kind, slot + sum(sizes[:i]), place)
        places[place] = jnp.int32(k)

    slots_of(cols, me, blocks, put)

    rows, lanes = iotas(half)
    for i, size in enumerate(sizes):
        diagonals = received[i][size * width :, :].astype(jnp.float32)
        for slot in range(size):
            base = slot * width
            triangle = received[i][base : base + half, :].astype(jnp.float32)
            upper = jnp.where(rows <= lanes, triangle, 0.0).astype(jnp.bfloat16)
            lower = jnp.where(rows < lanes, triangle.T, jnp.where(rows == lanes, diagonals[slot : slot + 1, :], 0.0))
            lower = lower.astype(jnp.bfloat16)
            corner = received[i][base + half : base + width, :]
            z_col = jnp.concatenate(
                [
                    jnp.concatenate([upper, corner], axis=1),
                    jnp.concatenate([jnp.zeros_like(lower), lower], axis=1),
                ],
                axis=0,
            )
            place = sum(sizes[:i]) + slot
            inner = jnp.dot(left[jnp.maximum(places[place], 0)], z_col, preferred_element_type=jnp.float32)
            product = jnp.dot(z_row[...], inner.astype(jnp.bfloat16), preferred_element_type=jnp.float32)
            results[place] = (-0.5 * product).astype(jnp.bfloat16)

    for slot in range(slots):
        k = places[slot]

        @pl.when(k >= 0)
        def _():
            pltpu.make_async_copy(results.at[slot], out.at[0, k], sems.at[slot]).start()

    for slot in range(slots):

        @pl.when(places[slot] >= 0)
        def _():
            pltpu.make_async_copy(results.at[slot], out.at[0, 0], sems.at[slot]).wait()


RIGHT_COST = (4*10**9,) * 3
LEFT_COST = 1
TINY = pl.CostEstimate(flops=1, bytes_accessed=1, transcendentals=0)
VMEM = pl.BlockSpec(memory_space=pltpu.VMEM)
SMEM = pl.BlockSpec(memory_space=pltpu.SMEM)
HBM = pl.BlockSpec(memory_space=pltpu.HBM)


def on_device(coupling_tiles, coupling_cols, row_blocks, factor_tiles):
    doms, panels = lax.axis_size("dom"), lax.axis_size("pan")
    blocks, width, _ = factor_tiles.shape
    _, count, _, _ = coupling_tiles.shape
    half, slots = width // 2, count - 1
    limit = pltpu.CompilerParams(vmem_limit_bytes=32 * 2**20)
    bf16 = lambda *shape: jax.ShapeDtypeStruct(shape, jnp.bfloat16)

    def flat(dom, panel):
        return dom * panels + panel

    straight = [(dom, dom ^ (doms // 2)) for dom in range(doms)]
    ends = (0, panels - 1)

    across = [
        (flat(dom, panel), flat(dom ^ (doms // 2), other_panel(panel, panels)))
        for dom in range(doms)
        for panel in range(panels)
        if panel not in ends
    ]
    at_ends = [(flat(dom, panel), flat(dom ^ (doms // 2), panel)) for dom in range(doms) for panel in ends]
    beside = [
        (flat(dom, panel), flat(dom, other_panel(panel, panels)))
        for dom in range(doms)
        for panel in range(panels)
        if panel not in ends
    ]

    far_cols = lax.ppermute(coupling_cols, ("dom", "pan"), across)

    own, z_row = pl.pallas_call(
        load_kernel,
        out_shape=(bf16(blocks, width, width), bf16(width, width)),
        in_specs=[SMEM, HBM],
        out_specs=(VMEM,) * 2,
        scratch_shapes=[pltpu.SemaphoreType.DMA] * 2,
        compiler_params=limit,
        cost_estimate=TINY,
        name="load",
    )(row_blocks, factor_tiles)

    def fill(kernel, sizes, *operands):
        return pl.pallas_call(
            kernel,
            out_shape=tuple(bf16(size * width + 16, half) for size in sizes),
            in_specs=[SMEM] + [VMEM] * (len(operands) - 1),
            out_specs=(VMEM,) * len(sizes),
            scratch_shapes=[pltpu.SMEM((sum(sizes) + 1,), jnp.int32)],
            compiler_params=limit,
            cost_estimate=TINY,
            name=kernel.__name__,
        )(*operands)

    far, relay = fill(far_kernel, (FAR, slots - FAR), far_cols, own)
    far, relay, given, cols = lax.optimization_barrier((far, relay, factor_tiles, coupling_cols))
    far = lax.ppermute(far, ("dom", "pan"), across)
    mate = lax.ppermute(given, "pan", [(panel, panel ^ 1) for panel in range(panels)])
    near_cols = lax.ppermute(cols, "dom", straight)
    relay = lax.ppermute(relay, ("dom", "pan"), beside)
    (near,) = fill(near_kernel, (NEAR,), near_cols, own, mate)
    near = lax.ppermute(near, "dom", straight)
    last, extra = fill(last_kernel, (LAST, 1), near_cols, own, mate, relay)
    last = lax.ppermute(last, "dom", straight)
    extra = lax.ppermute(extra, ("dom", "pan"), at_ends)
    steps = [
        ((IN_FAR,), (FAR,), (far,)),
        ((IN_NEAR,), (NEAR,), (near,)),
        ((IN_LAST, IN_EXTRA), (LAST, 1), (last, extra)),
    ]

    left = pl.pallas_call(
        left_kernel,
        out_shape=bf16(count, width, width),
        in_specs=[VMEM, VMEM],
        out_specs=VMEM,
        compiler_params=limit,
        cost_estimate=pl.CostEstimate(flops=LEFT_COST, bytes_accessed=1, transcendentals=0),
        name="left",
    )(z_row, coupling_tiles)

    out = None
    for i, (wanted, sizes, received) in enumerate(steps):
        operands = [coupling_cols, left, z_row, *received]
        total = sum(sizes)
        out = pl.pallas_call(
            functools.partial(right_kernel, wanted, sizes, blocks),
            out_shape=bf16(*coupling_tiles.shape),
            in_specs=[SMEM] + [VMEM] * (len(operands) - 1) + ([] if out is None else [HBM]),
            out_specs=HBM,
            scratch_shapes=[
                pltpu.VMEM((total, width, width), jnp.bfloat16),
                pltpu.SMEM((total + 1,), jnp.int32),
                pltpu.SemaphoreType.DMA((total,)),
            ],
            input_output_aliases={} if out is None else {len(operands): 0},
            compiler_params=limit,
            cost_estimate=pl.CostEstimate(flops=RIGHT_COST[i], bytes_accessed=1, transcendentals=0),
            name=f"right_{i}",
        )(*operands, *(() if out is None else (out,)))
    return out


def solution(mesh):
    return jax.shard_map(
        on_device,
        mesh=mesh,
        in_specs=(
            P(("dom", "pan"), None, None, None),
            P(("dom", "pan"), None),
            P(("dom", "pan")),
            P(("dom", "pan"), None, None),
        ),
        out_specs=P(("dom", "pan"), None, None, None),
        check_vma=False,
    )
```

```python
import functools

import jax
import jax.numpy as jnp
from jax import lax
from jax.experimental import pallas as pl
from jax.experimental.pallas import tpu as pltpu
from jax.sharding import PartitionSpec as P

NEAR, FAR, LAST = 5, 5, 2
IN_NEAR, IN_FAR, IN_LAST, IN_EXTRA = range(4)


def other_panel(panel, panels):
    return panel + 2 * (panel % 2) - 1


def slots_of(cols_ref, panel, blocks, put):
    near_used = jnp.int32(0)
    far_used = jnp.int32(0)
    for k in range(cols_ref.shape[1]):
        col = cols_ref[0, k]
        near = lax.div(col, 2 * blocks) == lax.div(panel, 2)
        used = jnp.where(near, near_used, far_used)
        room = jnp.where(near, NEAR, FAR)
        direct = used < room
        over = used - room
        message = jnp.where(direct, jnp.where(near, IN_NEAR, IN_FAR), jnp.where(over < LAST, IN_LAST, IN_EXTRA))
        put(k, col, message, jnp.where(direct, used, jnp.where(over < LAST, over, 0)))
        near_used = near_used + near.astype(jnp.int32)
        far_used = far_used + 1 - near.astype(jnp.int32)


def iotas(half):
    rows = lax.broadcasted_iota(jnp.int32, (half, half), 0)
    lanes = lax.broadcasted_iota(jnp.int32, (half, half), 1)
    return rows, lanes


def load_kernel(block, factors, own, z_row, sem, row_sem):
    copy = pltpu.make_async_copy(factors, own, sem)
    copy.start()
    row_copy = pltpu.make_async_copy(factors.at[block[0]], z_row, row_sem)
    row_copy.start()
    row_copy.wait()
    copy.wait()


def write_slot(out, slot, found, tile_part, width):
    half = width // 2
    rows, lanes = iotas(half)
    line = lax.broadcasted_iota(jnp.int32, (16, half), 0)
    head, tail = slice(0, half), slice(half, width)
    upper = tile_part(head, head).astype(jnp.float32)
    lower = tile_part(tail, tail).astype(jnp.float32)
    base = slot * width
    out[base : base + half, :] = jnp.where(rows <= lanes, upper, lower.T).astype(jnp.bfloat16)
    out[base + half : base + width, :] = tile_part(head, tail)
    diagonal = jnp.sum(jnp.where(rows == lanes, lower, 0.0), axis=0, keepdims=True)
    return jnp.where(line == slot, diagonal, found)


def chosen(index, own, mate):
    blocks = own.shape[0]
    mine = index < blocks
    block = jnp.where(mine, index, jnp.where(index < 2 * blocks, index - blocks, 0))
    return lambda rows, lanes: jnp.where(mine, own[block, rows, lanes], mate[block, rows, lanes])


def near_kernel(cols, own, mate, out, source):
    blocks, width, _ = own.shape
    me = lax.axis_index("pan")
    for slot in range(NEAR):
        source[slot] = jnp.int32(0)

    def put(k, col, message, slot):
        local = lax.rem(col, blocks) + jnp.where(lax.div(col, blocks) == me, 0, blocks)
        source[jnp.where(message == IN_NEAR, slot, NEAR)] = local

    slots_of(cols, me, blocks, put)
    found = jnp.zeros((16, width // 2), jnp.float32)
    for slot in range(NEAR):
        found = write_slot(out, slot, found, chosen(source[slot], own, mate), width)
    out[NEAR * width :, :] = found.astype(jnp.bfloat16)


def far_kernel(cols, own, far_out, relay_out, source):
    blocks, width, _ = own.shape
    relayed = relay_out.shape[0] // width
    total = FAR + relayed
    me = lax.axis_index("pan")
    there = me + 2 * lax.rem(me, 2) - 1
    for slot in range(total):
        source[slot] = jnp.int32(0)

    def put(k, col, message, slot):
        far = lax.div(col, blocks) == me
        place = jnp.where(message == IN_FAR, slot, FAR + slot)
        source[jnp.where(far, jnp.minimum(place, total), total)] = lax.rem(col, blocks)

    slots_of(cols, there, blocks, put)
    for out, first, size in ((far_out, 0, FAR), (relay_out, FAR, relayed)):
        found = jnp.zeros((16, width // 2), jnp.float32)
        for slot in range(size):
            found = write_slot(out, slot, found, chosen(source[first + slot], own, own), width)
        out[size * width :, :] = found.astype(jnp.bfloat16)


def last_kernel(cols, own, mate, relay, out, extra_out, source):
    blocks, width, _ = own.shape
    half = width // 2
    relayed = relay.shape[0] // width
    me = lax.axis_index("pan")
    for slot in range(LAST + 1):
        source[slot] = jnp.int32(0)

    def put(k, col, message, slot):
        local = lax.rem(col, blocks) + jnp.where(lax.div(col, blocks) == me, 0, blocks)
        near = lax.div(col, 2 * blocks) == lax.div(me, 2)
        place = jnp.where(message == IN_LAST, slot, jnp.where(message == IN_EXTRA, LAST, LAST + 1))
        source[place] = jnp.where(near, local, 2 * blocks)

    slots_of(cols, me, blocks, put)
    line = lax.broadcasted_iota(jnp.int32, (16, half), 0)
    found = jnp.zeros((16, half), jnp.float32)
    for slot in range(LAST):
        found = write_slot(out, slot, found, chosen(source[slot], own, mate), width)
    for slot in range(min(LAST, relayed)):
        base = slot * width
        theirs = source[slot] >= 2 * blocks
        out[base : base + width, :] = jnp.where(theirs, relay[base : base + width, :], out[base : base + width, :])
        found = jnp.where((line == slot) & theirs, relay[relayed * width :, :].astype(jnp.float32), found)
    out[LAST * width :, :] = found.astype(jnp.bfloat16)
    found = jnp.zeros((16, half), jnp.float32)
    found = write_slot(extra_out, 0, found, chosen(source[LAST], own, mate), width)
    extra_out[width:, :] = found.astype(jnp.bfloat16)


def first_right_kernel(wanted, sizes, blocks, cols, tiles, z_row, *rest):
    received, (out, left), scratch = rest[: len(wanted)], rest[len(wanted) : -3], rest[-3:]
    turned = z_row[...].astype(jnp.float32).T.astype(jnp.bfloat16)
    for k in range(tiles.shape[1]):
        left[k] = jnp.dot(turned, tiles[0, k], preferred_element_type=jnp.float32).astype(jnp.bfloat16)
    right_kernel(wanted, sizes, blocks, cols, left, z_row, *received, out, *scratch)


def right_kernel(wanted, sizes, blocks, cols, left, z_row, *rest):
    received = rest[: len(wanted)]
    out, results, places, sems = rest[-4:]
    slots, width, _ = results.shape
    half = width // 2
    me = lax.axis_index("pan")
    for slot in range(slots):
        places[slot] = jnp.int32(-1)

    def put(k, col, message, slot):
        place = jnp.int32(slots)
        for i, kind in enumerate(wanted):
            place = jnp.where(message == kind, slot + sum(sizes[:i]), place)
        places[place] = jnp.int32(k)

    slots_of(cols, me, blocks, put)

    rows, lanes = iotas(half)
    for i, size in enumerate(sizes):
        diagonals = received[i][size * width :, :].astype(jnp.float32)
        for slot in range(size):
            base = slot * width
            triangle = received[i][base : base + half, :].astype(jnp.float32)
            upper = jnp.where(rows <= lanes, triangle, 0.0).astype(jnp.bfloat16)
            lower = jnp.where(rows < lanes, triangle.T, jnp.where(rows == lanes, diagonals[slot : slot + 1, :], 0.0))
            lower = lower.astype(jnp.bfloat16)
            corner = received[i][base + half : base + width, :]
            z_col = jnp.concatenate(
                [
                    jnp.concatenate([upper, corner], axis=1),
                    jnp.concatenate([jnp.zeros_like(lower), lower], axis=1),
                ],
                axis=0,
            )
            place = sum(sizes[:i]) + slot
            inner = jnp.dot(left[jnp.maximum(places[place], 0)], z_col, preferred_element_type=jnp.float32)
            product = jnp.dot(z_row[...], inner.astype(jnp.bfloat16), preferred_element_type=jnp.float32)
            results[place] = (-0.5 * product).astype(jnp.bfloat16)

            @pl.when(places[place] >= 0)
            def _():
                pltpu.make_async_copy(results.at[place], out.at[0, places[place]], sems.at[place]).start()

    for slot in range(slots):

        @pl.when(places[slot] >= 0)
        def _():
            pltpu.make_async_copy(results.at[slot], out.at[0, 0], sems.at[slot]).wait()


FILL_COST = {far_kernel: 4 * 10**10}
RIGHT_COST = (4 * 10**9,) * 3
TINY = pl.CostEstimate(flops=1, bytes_accessed=1, transcendentals=0)
VMEM = pl.BlockSpec(memory_space=pltpu.VMEM)
SMEM = pl.BlockSpec(memory_space=pltpu.SMEM)
HBM = pl.BlockSpec(memory_space=pltpu.HBM)


def on_device(coupling_tiles, coupling_cols, row_blocks, factor_tiles):
    doms, panels = lax.axis_size("dom"), lax.axis_size("pan")
    blocks, width, _ = factor_tiles.shape
    _, count, _, _ = coupling_tiles.shape
    half, slots = width // 2, count - 1
    limit = pltpu.CompilerParams(vmem_limit_bytes=32 * 2**20)
    bf16 = lambda *shape: jax.ShapeDtypeStruct(shape, jnp.bfloat16)

    def flat(dom, panel):
        return dom * panels + panel

    straight = [(dom, dom ^ (doms // 2)) for dom in range(doms)]
    ends = (0, panels - 1)

    across = [
        (flat(dom, panel), flat(dom ^ (doms // 2), other_panel(panel, panels)))
        for dom in range(doms)
        for panel in range(panels)
        if panel not in ends
    ]
    at_ends = [(flat(dom, panel), flat(dom ^ (doms // 2), panel)) for dom in range(doms) for panel in ends]
    beside = [
        (flat(dom, panel), flat(dom, other_panel(panel, panels)))
        for dom in range(doms)
        for panel in range(panels)
        if panel not in ends
    ]

    far_cols = lax.ppermute(coupling_cols, ("dom", "pan"), across)

    own, z_row = pl.pallas_call(
        load_kernel,
        out_shape=(bf16(blocks, width, width), bf16(width, width)),
        in_specs=[SMEM, HBM],
        out_specs=(VMEM,) * 2,
        scratch_shapes=[pltpu.SemaphoreType.DMA] * 2,
        compiler_params=limit,
        cost_estimate=TINY,
        name="load",
    )(row_blocks, factor_tiles)

    def fill(kernel, sizes, *operands):
        return pl.pallas_call(
            kernel,
            out_shape=tuple(bf16(size * width + 16, half) for size in sizes),
            in_specs=[SMEM] + [VMEM] * (len(operands) - 1),
            out_specs=(VMEM,) * len(sizes),
            scratch_shapes=[pltpu.SMEM((sum(sizes) + 1,), jnp.int32)],
            compiler_params=limit,
            cost_estimate=pl.CostEstimate(flops=FILL_COST.get(kernel, 1), bytes_accessed=1, transcendentals=0),
            name=kernel.__name__,
        )(*operands)

    mate = lax.ppermute(factor_tiles, "pan", [(panel, panel ^ 1) for panel in range(panels)])
    far, relay = fill(far_kernel, (FAR, slots - FAR), far_cols, own)
    far, relay, cols = lax.optimization_barrier((far, relay, coupling_cols))
    far = lax.ppermute(far, ("dom", "pan"), across)
    near_cols = lax.ppermute(cols, "dom", straight)
    relay = lax.ppermute(relay, ("dom", "pan"), beside)
    (near,) = fill(near_kernel, (NEAR,), near_cols, own, mate)
    near = lax.ppermute(near, "dom", straight)
    last, extra = fill(last_kernel, (LAST, 1), near_cols, own, mate, relay)
    last = lax.ppermute(last, "dom", straight)
    extra = lax.ppermute(extra, ("dom", "pan"), at_ends)
    steps = [
        ((IN_FAR,), (FAR,), (far,)),
        ((IN_NEAR,), (NEAR,), (near,)),
        ((IN_LAST, IN_EXTRA), (LAST, 1), (last, extra)),
    ]

    out = left = None
    for i, (wanted, sizes, received) in enumerate(steps):
        begins = out is None
        total = sum(sizes)
        operands = [coupling_cols, coupling_tiles if begins else left, z_row, *received]
        results = pl.pallas_call(
            functools.partial(first_right_kernel if begins else right_kernel, wanted, sizes, blocks),
            out_shape=(bf16(*coupling_tiles.shape),) + ((bf16(count, width, width),) if begins else ()),
            in_specs=[SMEM] + [VMEM] * (len(operands) - 1) + ([] if begins else [HBM]),
            out_specs=(HBM, VMEM) if begins else (HBM,),
            scratch_shapes=[
                pltpu.VMEM((total, width, width), jnp.bfloat16),
                pltpu.SMEM((total + 1,), jnp.int32),
                pltpu.SemaphoreType.DMA((total,)),
            ],
            input_output_aliases={} if begins else {len(operands): 0},
            compiler_params=limit,
            cost_estimate=pl.CostEstimate(flops=RIGHT_COST[i], bytes_accessed=1, transcendentals=0),
            name=f"right_{i}",
        )(*operands, *(() if begins else (out,)))
        out = results[0]
        if begins:
            left = results[1]
    return out


def solution(mesh):
    return jax.shard_map(
        on_device,
        mesh=mesh,
        in_specs=(
            P(("dom", "pan"), None, None, None),
            P(("dom", "pan"), None),
            P(("dom", "pan")),
            P(("dom", "pan"), None, None),
        ),
        out_specs=P(("dom", "pan"), None, None, None),
        check_vma=False,
    )
```

```python
import functools

import jax
import jax.numpy as jnp
from jax import lax
from jax.experimental import pallas as pl
from jax.experimental.pallas import tpu as pltpu
from jax.sharding import PartitionSpec as P

NEAR, FAR, LAST = 5, 5, 2
IN_NEAR, IN_FAR, IN_LAST, IN_EXTRA = range(4)


def other_panel(panel, panels):
    return panel + 2 * (panel % 2) - 1


def slots_of(cols_ref, panel, blocks, put):
    near_used = jnp.int32(0)
    far_used = jnp.int32(0)
    for k in range(cols_ref.shape[1]):
        col = cols_ref[0, k]
        near = lax.div(col, 2 * blocks) == lax.div(panel, 2)
        used = jnp.where(near, near_used, far_used)
        room = jnp.where(near, NEAR, FAR)
        direct = used < room
        over = used - room
        message = jnp.where(direct, jnp.where(near, IN_NEAR, IN_FAR), jnp.where(over < LAST, IN_LAST, IN_EXTRA))
        put(k, col, message, jnp.where(direct, used, jnp.where(over < LAST, over, 0)))
        near_used = near_used + near.astype(jnp.int32)
        far_used = far_used + 1 - near.astype(jnp.int32)


def iotas(half):
    rows = lax.broadcasted_iota(jnp.int32, (half, half), 0)
    lanes = lax.broadcasted_iota(jnp.int32, (half, half), 1)
    return rows, lanes


def load_kernel(block, factors, own, z_row, sem, row_sem):
    copy = pltpu.make_async_copy(factors, own, sem)
    copy.start()
    row_copy = pltpu.make_async_copy(factors.at[block[0]], z_row, row_sem)
    row_copy.start()
    row_copy.wait()
    copy.wait()


def write_slot(out, slot, found, tile_part, width):
    half = width // 2
    rows, lanes = iotas(half)
    line = lax.broadcasted_iota(jnp.int32, (16, half), 0)
    head, tail = slice(0, half), slice(half, width)
    upper = tile_part(head, head).astype(jnp.float32)
    lower = tile_part(tail, tail).astype(jnp.float32)
    base = slot * width
    out[base : base + half, :] = jnp.where(rows <= lanes, upper, lower.T).astype(jnp.bfloat16)
    out[base + half : base + width, :] = tile_part(head, tail)
    diagonal = jnp.sum(jnp.where(rows == lanes, lower, 0.0), axis=0, keepdims=True)
    return jnp.where(line == slot, diagonal, found)


def chosen(index, own, mate):
    blocks = own.shape[0]
    mine = index < blocks
    block = jnp.where(mine, index, jnp.where(index < 2 * blocks, index - blocks, 0))
    return lambda rows, lanes: jnp.where(mine, own[block, rows, lanes], mate[block, rows, lanes])


def near_kernel(cols, own, mate, out, source):
    blocks, width, _ = own.shape
    me = lax.axis_index("pan")
    for slot in range(NEAR):
        source[slot] = jnp.int32(0)

    def put(k, col, message, slot):
        local = lax.rem(col, blocks) + jnp.where(lax.div(col, blocks) == me, 0, blocks)
        source[jnp.where(message == IN_NEAR, slot, NEAR)] = local

    slots_of(cols, me, blocks, put)
    found = jnp.zeros((16, width // 2), jnp.float32)
    for slot in range(NEAR):
        found = write_slot(out, slot, found, chosen(source[slot], own, mate), width)
    out[NEAR * width :, :] = found.astype(jnp.bfloat16)


def far_kernel(cols, own, far_out, relay_out, source):
    blocks, width, _ = own.shape
    relayed = relay_out.shape[0] // width
    total = FAR + relayed
    me = lax.axis_index("pan")
    there = me + 2 * lax.rem(me, 2) - 1
    for slot in range(total):
        source[slot] = jnp.int32(0)

    def put(k, col, message, slot):
        far = lax.div(col, blocks) == me
        place = jnp.where(message == IN_FAR, slot, FAR + slot)
        source[jnp.where(far, jnp.minimum(place, total), total)] = lax.rem(col, blocks)

    slots_of(cols, there, blocks, put)
    for out, first, size in ((far_out, 0, FAR), (relay_out, FAR, relayed)):
        found = jnp.zeros((16, width // 2), jnp.float32)
        for slot in range(size):
            found = write_slot(out, slot, found, chosen(source[first + slot], own, own), width)
        out[size * width :, :] = found.astype(jnp.bfloat16)


def last_kernel(cols, own, mate, relay, out, extra_out, source):
    blocks, width, _ = own.shape
    half = width // 2
    relayed = relay.shape[0] // width
    me = lax.axis_index("pan")
    for slot in range(LAST + 1):
        source[slot] = jnp.int32(0)

    def put(k, col, message, slot):
        local = lax.rem(col, blocks) + jnp.where(lax.div(col, blocks) == me, 0, blocks)
        near = lax.div(col, 2 * blocks) == lax.div(me, 2)
        place = jnp.where(message == IN_LAST, slot, jnp.where(message == IN_EXTRA, LAST, LAST + 1))
        source[place] = jnp.where(near, local, 2 * blocks)

    slots_of(cols, me, blocks, put)
    line = lax.broadcasted_iota(jnp.int32, (16, half), 0)
    found = jnp.zeros((16, half), jnp.float32)
    for slot in range(LAST):
        found = write_slot(out, slot, found, chosen(source[slot], own, mate), width)
    for slot in range(min(LAST, relayed)):
        base = slot * width
        theirs = source[slot] >= 2 * blocks
        out[base : base + width, :] = jnp.where(theirs, relay[base : base + width, :], out[base : base + width, :])
        found = jnp.where((line == slot) & theirs, relay[relayed * width :, :].astype(jnp.float32), found)
    out[LAST * width :, :] = found.astype(jnp.bfloat16)
    found = jnp.zeros((16, half), jnp.float32)
    found = write_slot(extra_out, 0, found, chosen(source[LAST], own, mate), width)
    extra_out[width:, :] = found.astype(jnp.bfloat16)


def first_right_kernel(wanted, sizes, blocks, cols, tiles, z_row, *rest):
    received, (out, left), scratch = rest[: len(wanted)], rest[len(wanted) : -3], rest[-3:]
    turned = z_row[...].astype(jnp.float32).T.astype(jnp.bfloat16)
    for k in range(tiles.shape[1]):
        left[k] = jnp.dot(turned, tiles[0, k], preferred_element_type=jnp.float32).astype(jnp.bfloat16)
    right_kernel(wanted, sizes, blocks, cols, left, z_row, *received, out, *scratch)


def right_kernel(wanted, sizes, blocks, cols, left, z_row, *rest):
    received = rest[: len(wanted)]
    out, results, places, sems = rest[-4:]
    slots, width, _ = results.shape
    half = width // 2
    me = lax.axis_index("pan")
    for slot in range(slots):
        places[slot] = jnp.int32(-1)

    def put(k, col, message, slot):
        place = jnp.int32(slots)
        for i, kind in enumerate(wanted):
            place = jnp.where(message == kind, slot + sum(sizes[:i]), place)
        places[place] = jnp.int32(k)

    slots_of(cols, me, blocks, put)

    rows, lanes = iotas(half)
    for i, size in enumerate(sizes):
        diagonals = received[i][size * width :, :].astype(jnp.float32)
        for slot in range(size):
            base = slot * width
            triangle = received[i][base : base + half, :].astype(jnp.float32)
            upper = jnp.where(rows <= lanes, triangle, 0.0).astype(jnp.bfloat16)
            lower = jnp.where(rows < lanes, triangle.T, jnp.where(rows == lanes, diagonals[slot : slot + 1, :], 0.0))
            lower = lower.astype(jnp.bfloat16)
            corner = received[i][base + half : base + width, :]
            z_col = jnp.concatenate(
                [
                    jnp.concatenate([upper, corner], axis=1),
                    jnp.concatenate([jnp.zeros_like(lower), lower], axis=1),
                ],
                axis=0,
            )
            place = sum(sizes[:i]) + slot
            inner = jnp.dot(left[jnp.maximum(places[place], 0)], z_col, preferred_element_type=jnp.float32)
            product = jnp.dot(z_row[...], inner.astype(jnp.bfloat16), preferred_element_type=jnp.float32)
            results[place] = (-0.5 * product).astype(jnp.bfloat16)

            @pl.when(places[place] >= 0)
            def _():
                pltpu.make_async_copy(results.at[place], out.at[0, places[place]], sems.at[place]).start()

    for slot in range(slots):

        @pl.when(places[slot] >= 0)
        def _():
            pltpu.make_async_copy(results.at[slot], out.at[0, 0], sems.at[slot]).wait()


FILL_COST = {far_kernel: 4 * 10**10}
RIGHT_COST = (4 * 10**9,) * 3
TINY = pl.CostEstimate(flops=1, bytes_accessed=1, transcendentals=0)
VMEM = pl.BlockSpec(memory_space=pltpu.VMEM)
SMEM = pl.BlockSpec(memory_space=pltpu.SMEM)
HBM = pl.BlockSpec(memory_space=pltpu.HBM)


def on_device(coupling_tiles, coupling_cols, row_blocks, factor_tiles):
    doms, panels = lax.axis_size("dom"), lax.axis_size("pan")
    blocks, width, _ = factor_tiles.shape
    _, count, _, _ = coupling_tiles.shape
    half, slots = width // 2, count - 1
    limit = pltpu.CompilerParams(vmem_limit_bytes=32 * 2**20)
    bf16 = lambda *shape: jax.ShapeDtypeStruct(shape, jnp.bfloat16)

    def flat(dom, panel):
        return dom * panels + panel

    straight = [(dom, dom ^ (doms // 2)) for dom in range(doms)]
    ends = (0, panels - 1)

    across = [
        (flat(dom, panel), flat(dom ^ (doms // 2), other_panel(panel, panels)))
        for dom in range(doms)
        for panel in range(panels)
        if panel not in ends
    ]
    at_ends = [(flat(dom, panel), flat(dom ^ (doms // 2), panel)) for dom in range(doms) for panel in ends]
    beside = [
        (flat(dom, panel), flat(dom, other_panel(panel, panels)))
        for dom in range(doms)
        for panel in range(panels)
        if panel not in ends
    ]

    far_cols = lax.ppermute(coupling_cols, ("dom", "pan"), across)

    own, z_row = pl.pallas_call(
        load_kernel,
        out_shape=(bf16(blocks, width, width), bf16(width, width)),
        in_specs=[SMEM, HBM],
        out_specs=(VMEM,) * 2,
        scratch_shapes=[pltpu.SemaphoreType.DMA] * 2,
        compiler_params=limit,
        cost_estimate=TINY,
        name="load",
    )(row_blocks, pltpu.with_memory_space_constraint(factor_tiles, pltpu.HBM))

    def fill(kernel, sizes, *operands):
        return pl.pallas_call(
            kernel,
            out_shape=tuple(bf16(size * width + 16, half) for size in sizes),
            in_specs=[SMEM] + [VMEM] * (len(operands) - 1),
            out_specs=(VMEM,) * len(sizes),
            scratch_shapes=[pltpu.SMEM((sum(sizes) + 1,), jnp.int32)],
            compiler_params=limit,
            cost_estimate=pl.CostEstimate(flops=FILL_COST.get(kernel, 1), bytes_accessed=1, transcendentals=0),
            name=kernel.__name__,
        )(*operands)

    mate = lax.ppermute(factor_tiles, "pan", [(panel, panel ^ 1) for panel in range(panels)])
    own, cols = lax.optimization_barrier((own, coupling_cols))
    far, relay = fill(far_kernel, (FAR, slots - FAR), far_cols, own)
    far = lax.ppermute(far, ("dom", "pan"), across)
    near_cols = lax.ppermute(cols, "dom", straight)
    relay = lax.ppermute(relay, ("dom", "pan"), beside)
    (near,) = fill(near_kernel, (NEAR,), near_cols, own, mate)
    near = lax.ppermute(near, "dom", straight)
    last, extra = fill(last_kernel, (LAST, 1), near_cols, own, mate, relay)
    last = lax.ppermute(last, "dom", straight)
    extra = lax.ppermute(extra, ("dom", "pan"), at_ends)
    steps = [
        ((IN_FAR,), (FAR,), (far,)),
        ((IN_NEAR,), (NEAR,), (near,)),
        ((IN_LAST, IN_EXTRA), (LAST, 1), (last, extra)),
    ]

    out = left = None
    for i, (wanted, sizes, received) in enumerate(steps):
        begins = out is None
        total = sum(sizes)
        operands = [coupling_cols, coupling_tiles if begins else left, z_row, *received]
        results = pl.pallas_call(
            functools.partial(first_right_kernel if begins else right_kernel, wanted, sizes, blocks),
            out_shape=(bf16(*coupling_tiles.shape),) + ((bf16(count, width, width),) if begins else ()),
            in_specs=[SMEM] + [VMEM] * (len(operands) - 1) + ([] if begins else [HBM]),
            out_specs=(HBM, VMEM) if begins else (HBM,),
            scratch_shapes=[
                pltpu.VMEM((total, width, width), jnp.bfloat16),
                pltpu.SMEM((total + 1,), jnp.int32),
                pltpu.SemaphoreType.DMA((total,)),
            ],
            input_output_aliases={} if begins else {len(operands): 0},
            compiler_params=limit,
            cost_estimate=pl.CostEstimate(flops=RIGHT_COST[i], bytes_accessed=1, transcendentals=0),
            name=f"right_{i}",
        )(*operands, *(() if begins else (out,)))
        out = results[0]
        if begins:
            left = results[1]
    return out


def solution(mesh):
    return jax.shard_map(
        on_device,
        mesh=mesh,
        in_specs=(
            P(("dom", "pan"), None, None, None),
            P(("dom", "pan"), None),
            P(("dom", "pan")),
            P(("dom", "pan"), None, None),
        ),
        out_specs=P(("dom", "pan"), None, None, None),
        check_vma=False,
    )
```
